32 devices in a mesh: ctx: 16 (over z, y, core), kvh: 2 (over x).
Axes of the slice: x: 2, y: 2, z: 4, core: 2. Of those that a mesh axis runs over, the one named last changes fastest.
Arguments:
- queries: bfloat16 [4096, 64, 128], P('ctx', 'kvh'), may hold values from -110 to 110
- key_value: bfloat16 [2, 4096, 8, 128], P(None, 'ctx', 'kvh'), may hold values from -5 to 5
- span_table: int32 [32], replicated, may hold values from 0 to 31, as said below
Outputs:
- attended: bfloat16 [4096, 8192], P(('ctx', 'kvh'))
The draws below stay inside these ranges and needn't reach their ends.
Inputs may be any that keep to these rules, and one draw needn't show every extreme that they name: `span_table`: entries 2 d and 2 d + 1 are the spans of ctx index d: the first below 16, the second 16 or above; every span of 0 to 31 appears exactly once.
All inputs are finite; a program needn't handle non-finite values.
Results may differ from the reference program's by a relative error of at most 0.0065.
Values may be sent and summed in bfloat16 or wider, within the bound.
A program may use at most 64 MiB of HBM per device.

```python
import jax
import jax.numpy as jnp
from jax import lax

QH = 64
KVH = 8
HD = 128
CH = 128
STEPS = 4
TOKENS = 4096
N_CTX = 16


def base_keys(key):
    base = jax.random.normal(jax.random.fold_in(key, 11), (TOKENS, KVH, HD), jnp.float32)
    return jnp.clip(base, -4.5, 4.5)


def draw_key_value(key, part):
    base = base_keys(key)
    keys = base
    vals = jnp.clip(jax.random.normal(jax.random.fold_in(key, 14), (TOKENS, KVH, HD), jnp.float32), -4.5, 4.5)
    return jnp.stack([keys, vals]).astype(jnp.bfloat16)


def draw_queries(key, part):
    drawn = jnp.clip(jax.random.normal(jax.random.fold_in(key, 13), (TOKENS, QH, HD), jnp.float32), -4.5, 4.5)
    result = drawn
    return result.astype(jnp.bfloat16)


def draw_span_table(key, part):
    early = jax.random.permutation(jax.random.fold_in(key, 21), N_CTX).astype(jnp.int32)
    late = N_CTX + jax.random.permutation(jax.random.fold_in(key, 22), N_CTX).astype(jnp.int32)
    return jnp.stack([early, late], axis=1).reshape(2 * N_CTX).astype(jnp.int32)


def setup_inputs(seed: int = 0) -> dict:
    arg_keys = jax.random.split(jax.random.key(seed), 4)
    queries = draw_queries(jax.random.fold_in(arg_keys[3], 71), 0)
    key_value = draw_key_value(jax.random.fold_in(arg_keys[3], 71), 0)
    span_table = draw_span_table(jax.random.fold_in(arg_keys[3], 71), 0)
    return {"queries": queries, "key_value": key_value, "span_table": span_table}


def reference(queries, key_value, span_table):
    rows = 2 * CH
    group = QH // KVH
    scale = 1.0 / (HD ** 0.5)
    offsets = jnp.arange(CH, dtype=jnp.int32)
    positions = (span_table[:, None] * CH + offsets[None, :]).reshape(N_CTX, rows).astype(jnp.int32)
    qall = queries.reshape(N_CTX, rows, KVH, group, HD)
    kall = key_value[0].reshape(N_CTX, rows, KVH, HD)
    vall = key_value[1].reshape(N_CTX, rows, KVH, HD)

    def one_device(dev):
        qdev = lax.dynamic_index_in_dim(qall, dev, 0, keepdims=False).astype(jnp.float32)
        qpos = lax.dynamic_index_in_dim(positions, dev, 0, keepdims=False)
        maxima = []
        outs = []
        sums = []
        for dist in range(STEPS):
            src = ((dev - dist) % N_CTX).astype(jnp.int32)
            kdev = lax.dynamic_index_in_dim(kall, src, 0, keepdims=False).astype(jnp.float32)
            vdev = lax.dynamic_index_in_dim(vall, src, 0, keepdims=False).astype(jnp.float32)
            kpos = lax.dynamic_index_in_dim(positions, src, 0, keepdims=False)
            scores = jnp.einsum("qghd,kgd->ghqk", qdev, kdev) * scale
            visible = (kpos[None, :] <= qpos[:, None])[None, None]
            masked = jnp.where(visible, scores, -jnp.inf)
            block_max = jnp.maximum(jnp.max(masked, axis=-1), jnp.float32(-1e30))
            weight = jnp.exp(masked - block_max[..., None])
            weight_low = weight.astype(jnp.bfloat16).astype(jnp.float32)
            sums.append(jnp.sum(weight, axis=-1))
            outs.append(jnp.einsum("ghqk,kgd->ghqd", weight_low, vdev))
            maxima.append(block_max)
        top = maxima[0]
        for m in maxima[1:]:
            top = jnp.maximum(top, m)
        numer = jnp.zeros_like(outs[0])
        denom = jnp.zeros_like(sums[0])
        for m, o, s in zip(maxima, outs, sums):
            factor = jnp.exp(m - top)
            numer = numer + factor[..., None] * o
            denom = denom + factor * s
        result = numer / denom[..., None]
        return jnp.transpose(result, (2, 0, 1, 3)).reshape(rows, QH * HD).astype(jnp.bfloat16)

    stacked = lax.map(one_device, jnp.arange(N_CTX, dtype=jnp.int32))
    return stacked.reshape(TOKENS, QH * HD)
```

```python
import functools
import math

import jax
import jax.numpy as jnp
from jax import lax
from jax.experimental import pallas as pl
from jax.experimental.pallas import tpu as pltpu
from jax.sharding import PartitionSpec as P

STEPS = 4
MESH = pl.DeviceIdType.MESH
LOW = -1e30
TILES = 4


def kernel(
    cycle,
    table_ref,
    q_hbm,
    kv_hbm,
    out_ref,
    q_in,
    kv_in,
    wide,
    qg,
    kvbuf,
    result,
    outbuf,
    load_sem,
    near_send,
    far_send,
    pass_send,
    kv_recv,
    out_send,
    out_recv,
    keep_sem,
):
    me = lax.axis_index("ctx")
    side = lax.axis_index("kvh")
    core = lax.rem(me, 2)
    rows, heads, hd = q_in.shape
    kvs = kvbuf.shape[0]
    group = heads // kvs
    span = rows // 2
    tile_q = span // TILES
    tile_rows = tile_q * group
    width = group * hd
    factor = math.log2(math.e) / math.sqrt(hd)

    def ahead(n):
        return lax.rem(me + n + cycle, cycle)

    partner = me + 1 - 2 * core
    other = 1 - side

    load_kv = pltpu.make_async_copy(kv_hbm, kv_in, load_sem.at[0])
    load_kv.start()
    load_q = pltpu.make_async_copy(q_hbm, q_in, load_sem.at[1])
    load_q.start()

    barrier = pltpu.get_barrier_semaphore()
    pl.semaphore_signal(barrier, inc=1, device_id=(ahead(-2), side), device_id_type=MESH)
    pl.semaphore_signal(barrier, inc=1, device_id=(partner, side), device_id_type=MESH)
    pl.semaphore_signal(barrier, inc=1, device_id=(me, other), device_id_type=MESH)

    @pl.when(core == 0)
    def _():
        pl.semaphore_signal(barrier, inc=1, device_id=(ahead(-3), side), device_id_type=MESH)

    load_kv.wait()
    for part in range(2):
        wide[part] = kv_in[part].astype(jnp.float32)
    for g in range(kvs):
        for part in range(2):
            for s in range(2):
                kvbuf[g, part, s, 0] = wide[
                    part, pl.ds(s * span * kvs + g, span, stride=kvs), :
                ].astype(jnp.bfloat16)

    pl.semaphore_wait(barrier, 3 + core)

    far_slot = 1 + 2 * core
    pass_slot = 3 - 2 * core
    far_device = ahead(1 + 2 * core)

    def send_near(g):
        return pltpu.make_async_remote_copy(
            src_ref=kvbuf.at[g, :, :, 0],
            dst_ref=kvbuf.at[g, :, :, 2],
            send_sem=near_send.at[g],
            recv_sem=kv_recv.at[g, 2],
            device_id=(ahead(2), side),
            device_id_type=MESH,
        )

    def send_far(g):
        return pltpu.make_async_remote_copy(
            src_ref=kvbuf.at[g, :, :, 0],
            dst_ref=kvbuf.at[g, :, :, far_slot],
            send_sem=far_send.at[g],
            recv_sem=kv_recv.at[g, far_slot],
            device_id=(far_device, side),
            device_id_type=MESH,
        )

    def send_pass(g):
        return pltpu.make_async_remote_copy(
            src_ref=kvbuf.at[g, :, :, 2],
            dst_ref=kvbuf.at[g, :, :, pass_slot],
            send_sem=pass_send.at[g],
            recv_sem=kv_recv.at[g, pass_slot],
            device_id=(partner, side),
            device_id_type=MESH,
        )

    def arrival(g, slot):
        return pltpu.make_async_remote_copy(
            src_ref=kvbuf.at[g, :, :, 0],
            dst_ref=kvbuf.at[g, :, :, slot],
            send_sem=near_send.at[g],
            recv_sem=kv_recv.at[g, slot],
            device_id=(partner, side),
            device_id_type=MESH,
        )

    def columns(owner, g):
        return pl.ds(pl.multiple_of((owner * kvs + g) * width, width), width)

    def send_out(g):
        return pltpu.make_async_remote_copy(
            src_ref=outbuf.at[0, g],
            dst_ref=out_ref.at[:, columns(side, g)],
            send_sem=out_send.at[g],
            recv_sem=out_recv.at[g],
            device_id=(me, other),
            device_id_type=MESH,
        )

    def take_out(g):
        return pltpu.make_async_remote_copy(
            src_ref=outbuf.at[0, g],
            dst_ref=out_ref.at[:, columns(other, g)],
            send_sem=out_send.at[g],
            recv_sem=out_recv.at[g],
            device_id=(me, other),
            device_id_type=MESH,
        )

    def keep_out(g):
        return pltpu.make_async_copy(
            outbuf.at[1, g], out_ref.at[:, columns(side, g)], keep_sem.at[g]
        )

    for g in range(kvs):
        send_near(g).start()
        send_far(g).start()

    load_q.wait()
    for t in range(2 * TILES):
        block = q_in[t * tile_q : (t + 1) * tile_q].astype(jnp.float32)
        for g in range(kvs):
            qg[g, t * tile_rows : (t + 1) * tile_rows, :] = (
                block[:, g * group : (g + 1) * group, :]
                .reshape(tile_rows, hd)
                .astype(jnp.bfloat16)
            )

    biases = []
    for s in range(2):
        mine = table_ref[2 * me + s]
        biases.append(
            [None]
            + [
                jnp.where(table_ref[2 * ahead(-b) + s] < mine, 0.0, LOW).astype(jnp.float32)
                for b in range(1, STEPS)
            ]
        )

    def attend(g, late, slot):
        spans = 2 if late else 1
        keys = spans * STEPS * span

        def one(t, carry):
            start = pl.multiple_of(t * tile_rows, tile_rows)
            q = qg[g, pl.ds((span * group if late else 0) + start, tile_rows), :]
            k = kvbuf[g, 0, :spans].reshape(keys, hd)
            v = kvbuf[g, 1, :spans].reshape(keys, hd)
            scores = lax.dot_general(
                q, k, (((1,), (1,)), ((), ())), preferred_element_type=jnp.float32
            )
            parts = []
            for s in range(spans):
                for b in range(STEPS):
                    part = scores[:, (s * STEPS + b) * span : (s * STEPS + b + 1) * span]
                    if s == spans - 1:
                        if b == 0:
                            row = lax.broadcasted_iota(jnp.int32, part.shape, 0) // group
                            col = lax.broadcasted_iota(jnp.int32, part.shape, 1)
                            part = jnp.where(col <= row + t * tile_q, part, LOW)
                        else:
                            part = part + biases[s][b]
                    parts.append(part)
            top = functools.reduce(jnp.maximum, parts)
            top = jnp.max(top, axis=-1, keepdims=True)
            weights = jnp.concatenate(
                [jnp.exp2((part - top) * factor).astype(jnp.bfloat16) for part in parts], axis=1
            )
            both = jnp.dot(
                weights,
                jnp.concatenate([v, jnp.ones_like(v)], axis=1),
                preferred_element_type=jnp.float32,
            )
            result[pl.ds(start, tile_rows), :] = both[:, :hd] / both[:, hd:]
            first = pl.multiple_of(t * tile_q, tile_q)
            for h in range(group):
                outbuf[slot, g, pl.ds(first, tile_q), h * hd : (h + 1) * hd] = result[
                    pl.ds(start + h, tile_q, stride=group), :
                ].astype(jnp.bfloat16)
            return carry

        lax.fori_loop(0, TILES, one, 0)

    def compute(g, slot):
        late = jnp.where(slot == 0, other, side)

        @pl.when(late == 1)
        def _():
            attend(g, True, slot)

        @pl.when(late == 0)
        def _():
            attend(g, False, slot)

    arrival(0, 2).wait_recv()
    send_pass(0).start()

    def step(i, carry):
        g = i // 2
        slot = lax.rem(i, 2)

        @pl.when(slot == 0)
        def _():
            arrival(g, 1).wait_recv()
            arrival(g, 3).wait_recv()

        @pl.when(jnp.logical_and(slot == 1, g < kvs - 1))
        def _():
            arrival(g + 1, 2).wait_recv()
            send_pass(g + 1).start()

        compute(g, slot)

        @pl.when(slot == 0)
        def _():
            send_out(g).start()

        @pl.when(slot == 1)
        def _():
            keep_out(g).start()

        return carry

    lax.fori_loop(0, 2 * kvs, step, 0)

    for g in range(kvs):
        keep_out(g).wait()
        send_near(g).wait_send()
        send_far(g).wait_send()
        send_pass(g).wait_send()
    for g in range(kvs):
        send_out(g).wait_send()
        take_out(g).wait_recv()


def body(queries, key_value, span_table):
    rows, heads, hd = queries.shape
    kvs = key_value.shape[2]
    group = heads // kvs
    span = rows // 2
    cycle = lax.axis_size("ctx")
    sides = lax.axis_size("kvh")
    flat = key_value.reshape(2, rows * kvs, hd)
    dma = pltpu.SemaphoreType.DMA
    flops = 3 * 2 * 2 * span * heads * STEPS * span * hd
    return pl.pallas_call(
        functools.partial(kernel, cycle),
        out_shape=jax.ShapeDtypeStruct((rows // sides, sides * heads * hd), jnp.bfloat16),
        in_specs=[
            pl.BlockSpec(memory_space=pltpu.SMEM),
            pl.BlockSpec(memory_space=pl.ANY),
            pl.BlockSpec(memory_space=pl.ANY),
        ],
        out_specs=pl.BlockSpec(memory_space=pl.ANY),
        scratch_shapes=[
            pltpu.VMEM((rows, heads, hd), jnp.bfloat16),
            pltpu.VMEM((2, rows * kvs, hd), jnp.bfloat16),
            pltpu.VMEM((2, rows * kvs, hd), jnp.float32),
            pltpu.VMEM((kvs, rows * group, hd), jnp.bfloat16),
            pltpu.VMEM((kvs, 2, 2, STEPS, span, hd), jnp.bfloat16),
            pltpu.VMEM((span * group, hd), jnp.float32),
            pltpu.VMEM((2, kvs, span, group * hd), jnp.bfloat16),
            dma((2,)),
            dma((kvs,)),
            dma((kvs,)),
            dma((kvs,)),
            dma((kvs, STEPS)),
            dma((kvs,)),
            dma((kvs,)),
            dma((kvs,)),
        ],
        compiler_params=pltpu.CompilerParams(
            collective_id=0, has_side_effects=True, vmem_limit_bytes=40 * 1024 * 1024
        ),
        cost_estimate=pl.CostEstimate(
            flops=flops, bytes_accessed=5 * 1024 * 1024, transcendentals=flops // (4 * hd)
        ),
    )(span_table, queries, flat)


def solution(mesh):
    in_specs = (P("ctx", "kvh", None), P(None, "ctx", "kvh", None), P())
    out_specs = P(("ctx", "kvh"), None)
    return jax.shard_map(body, mesh=mesh, in_specs=in_specs, out_specs=out_specs, check_vma=False)
```

```python
import functools
import math

import jax
import jax.numpy as jnp
from jax import lax
from jax.experimental import pallas as pl
from jax.experimental.pallas import tpu as pltpu
from jax.sharding import PartitionSpec as P

STEPS = 4
MESH = pl.DeviceIdType.MESH
LOW = -1e30
TILES = 4


def kernel(
    cycle,
    table_hbm,
    q_hbm,
    kv_hbm,
    out_ref,
    table_ref,
    q_in,
    kv_in,
    wide,
    qg,
    kvbuf,
    result,
    outbuf,
    load_sem,
    near_send,
    far_send,
    pass_send,
    kv_recv,
    out_send,
    out_recv,
    keep_sem,
):
    me = lax.axis_index("ctx")
    side = lax.axis_index("kvh")
    core = lax.rem(me, 2)
    rows, heads, hd = q_in.shape
    kvs = kvbuf.shape[0]
    group = heads // kvs
    span = rows // 2
    tile_q = span // TILES
    tile_rows = tile_q * group
    width = group * hd
    factor = math.log2(math.e) / math.sqrt(hd)

    def ahead(n):
        return lax.rem(me + n + cycle, cycle)

    partner = me + 1 - 2 * core
    other = 1 - side

    load_kv = pltpu.make_async_copy(kv_hbm, kv_in, load_sem.at[0])
    load_kv.start()
    load_q = pltpu.make_async_copy(q_hbm, q_in, load_sem.at[1])
    load_q.start()
    load_table = pltpu.make_async_copy(table_hbm, table_ref, load_sem.at[2])
    load_table.start()

    barrier = pltpu.get_barrier_semaphore()
    pl.semaphore_signal(barrier, inc=1, device_id=(ahead(-2), side), device_id_type=MESH)
    pl.semaphore_signal(barrier, inc=1, device_id=(partner, side), device_id_type=MESH)
    pl.semaphore_signal(barrier, inc=1, device_id=(me, other), device_id_type=MESH)

    @pl.when(core == 0)
    def _():
        pl.semaphore_signal(barrier, inc=1, device_id=(ahead(-3), side), device_id_type=MESH)

    load_kv.wait()
    for part in range(2):
        wide[part] = kv_in[part].astype(jnp.float32)
    for g in range(kvs):
        for part in range(2):
            for s in range(2):
                kvbuf[g, part, s, 0] = wide[
                    part, pl.ds(s * span * kvs + g, span, stride=kvs), :
                ].astype(jnp.bfloat16)

    pl.semaphore_wait(barrier, 3 + core)

    far_slot = 1 + 2 * core
    pass_slot = 3 - 2 * core
    far_device = ahead(1 + 2 * core)

    def send_near(g):
        return pltpu.make_async_remote_copy(
            src_ref=kvbuf.at[g, :, :, 0],
            dst_ref=kvbuf.at[g, :, :, 2],
            send_sem=near_send.at[g],
            recv_sem=kv_recv.at[g, 2],
            device_id=(ahead(2), side),
            device_id_type=MESH,
        )

    def send_far(g):
        return pltpu.make_async_remote_copy(
            src_ref=kvbuf.at[g, :, :, 0],
            dst_ref=kvbuf.at[g, :, :, far_slot],
            send_sem=far_send.at[g],
            recv_sem=kv_recv.at[g, far_slot],
            device_id=(far_device, side),
            device_id_type=MESH,
        )

    def send_pass(g):
        return pltpu.make_async_remote_copy(
            src_ref=kvbuf.at[g, :, :, 2],
            dst_ref=kvbuf.at[g, :, :, pass_slot],
            send_sem=pass_send.at[g],
            recv_sem=kv_recv.at[g, pass_slot],
            device_id=(partner, side),
            device_id_type=MESH,
        )

    def arrival(g, slot):
        return pltpu.make_async_remote_copy(
            src_ref=kvbuf.at[g, :, :, 0],
            dst_ref=kvbuf.at[g, :, :, slot],
            send_sem=near_send.at[g],
            recv_sem=kv_recv.at[g, slot],
            device_id=(partner, side),
            device_id_type=MESH,
        )

    def columns(owner, g):
        return pl.ds(pl.multiple_of((owner * kvs + g) * width, width), width)

    def send_out(g):
        return pltpu.make_async_remote_copy(
            src_ref=outbuf.at[0, g],
            dst_ref=out_ref.at[:, columns(side, g)],
            send_sem=out_send.at[g],
            recv_sem=out_recv.at[g],
            device_id=(me, other),
            device_id_type=MESH,
        )

    def take_out(g):
        return pltpu.make_async_remote_copy(
            src_ref=outbuf.at[0, g],
            dst_ref=out_ref.at[:, columns(other, g)],
            send_sem=out_send.at[g],
            recv_sem=out_recv.at[g],
            device_id=(me, other),
            device_id_type=MESH,
        )

    def keep_out(g):
        return pltpu.make_async_copy(
            outbuf.at[1, g], out_ref.at[:, columns(side, g)], keep_sem.at[g]
        )

    for g in range(kvs):
        send_near(g).start()
        send_far(g).start()

    load_q.wait()
    for t in range(2 * TILES):
        block = q_in[t * tile_q : (t + 1) * tile_q].astype(jnp.float32)
        for g in range(kvs):
            qg[g, t * tile_rows : (t + 1) * tile_rows, :] = (
                block[:, g * group : (g + 1) * group, :]
                .reshape(tile_rows, hd)
                .astype(jnp.bfloat16)
            )

    load_table.wait()
    biases = []
    for s in range(2):
        mine = table_ref[2 * me + s]
        biases.append(
            [None]
            + [
                jnp.where(table_ref[2 * ahead(-b) + s] < mine, 0.0, LOW).astype(jnp.float32)
                for b in range(1, STEPS)
            ]
        )

    def attend(g, late, slot):
        spans = 2 if late else 1
        keys = spans * STEPS * span

        def one(t, carry):
            start = pl.multiple_of(t * tile_rows, tile_rows)
            q = qg[g, pl.ds((span * group if late else 0) + start, tile_rows), :]
            k = kvbuf[g, 0, :spans].reshape(keys, hd)
            v = kvbuf[g, 1, :spans].reshape(keys, hd)
            scores = lax.dot_general(
                q, k, (((1,), (1,)), ((), ())), preferred_element_type=jnp.float32
            )
            parts = []
            for s in range(spans):
                for b in range(STEPS):
                    part = scores[:, (s * STEPS + b) * span : (s * STEPS + b + 1) * span]
                    if s == spans - 1:
                        if b == 0:
                            row = lax.broadcasted_iota(jnp.int32, part.shape, 0) // group
                            col = lax.broadcasted_iota(jnp.int32, part.shape, 1)
                            part = jnp.where(col <= row + t * tile_q, part, LOW)
                        else:
                            part = part + biases[s][b]
                    parts.append(part)
            top = functools.reduce(jnp.maximum, parts)
            top = jnp.max(top, axis=-1, keepdims=True)
            weights = jnp.concatenate(
                [jnp.exp2((part - top) * factor).astype(jnp.bfloat16) for part in parts], axis=1
            )
            both = jnp.dot(
                weights,
                jnp.concatenate([v, jnp.ones_like(v)], axis=1),
                preferred_element_type=jnp.float32,
            )
            result[pl.ds(start, tile_rows), :] = both[:, :hd] / both[:, hd:]
            first = pl.multiple_of(t * tile_q, tile_q)
            for h in range(group):
                outbuf[slot, g, pl.ds(first, tile_q), h * hd : (h + 1) * hd] = result[
                    pl.ds(start + h, tile_q, stride=group), :
                ].astype(jnp.bfloat16)
            return carry

        lax.fori_loop(0, TILES, one, 0, unroll=True)

    def compute(g, slot):
        late = jnp.where(slot == 0, other, side)

        @pl.when(late == 1)
        def _():
            attend(g, True, slot)

        @pl.when(late == 0)
        def _():
            attend(g, False, slot)

    arrival(0, 2).wait_recv()
    send_pass(0).start()

    def step(i, carry):
        g = i // 2
        slot = lax.rem(i, 2)

        @pl.when(slot == 0)
        def _():
            arrival(g, 1).wait_recv()
            arrival(g, 3).wait_recv()

        @pl.when(jnp.logical_and(slot == 1, g < kvs - 1))
        def _():
            arrival(g + 1, 2).wait_recv()
            send_pass(g + 1).start()

        compute(g, slot)

        @pl.when(slot == 0)
        def _():
            send_out(g).start()

        @pl.when(slot == 1)
        def _():
            keep_out(g).start()

        return carry

    lax.fori_loop(0, 2 * kvs, step, 0)

    for g in range(kvs):
        keep_out(g).wait()
        send_near(g).wait_send()
        send_far(g).wait_send()
        send_pass(g).wait_send()
    for g in range(kvs):
        send_out(g).wait_send()
        take_out(g).wait_recv()


def body(queries, key_value, span_table):
    rows, heads, hd = queries.shape
    kvs = key_value.shape[2]
    group = heads // kvs
    span = rows // 2
    cycle = lax.axis_size("ctx")
    sides = lax.axis_size("kvh")
    flat = key_value.reshape(2, rows * kvs, hd)
    dma = pltpu.SemaphoreType.DMA
    flops = 3 * 2 * 2 * span * heads * STEPS * span * hd
    return pl.pallas_call(
        functools.partial(kernel, cycle),
        out_shape=jax.ShapeDtypeStruct((rows // sides, sides * heads * hd), jnp.bfloat16),
        in_specs=[
            pl.BlockSpec(memory_space=pl.ANY),
            pl.BlockSpec(memory_space=pl.ANY),
            pl.BlockSpec(memory_space=pl.ANY),
        ],
        out_specs=pl.BlockSpec(memory_space=pl.ANY),
        scratch_shapes=[
            pltpu.SMEM(span_table.shape, jnp.int32),
            pltpu.VMEM((rows, heads, hd), jnp.bfloat16),
            pltpu.VMEM((2, rows * kvs, hd), jnp.bfloat16),
            pltpu.VMEM((2, rows * kvs, hd), jnp.float32),
            pltpu.VMEM((kvs, rows * group, hd), jnp.bfloat16),
            pltpu.VMEM((kvs, 2, 2, STEPS, span, hd), jnp.bfloat16),
            pltpu.VMEM((span * group, hd), jnp.float32),
            pltpu.VMEM((2, kvs, span, group * hd), jnp.bfloat16),
            dma((3,)),
            dma((kvs,)),
            dma((kvs,)),
            dma((kvs,)),
            dma((kvs, STEPS)),
            dma((kvs,)),
            dma((kvs,)),
            dma((kvs,)),
        ],
        compiler_params=pltpu.CompilerParams(
            collective_id=0, has_side_effects=True, vmem_limit_bytes=60 * 1024 * 1024
        ),
        cost_estimate=pl.CostEstimate(
            flops=flops, bytes_accessed=5 * 1024 * 1024, transcendentals=flops // (4 * hd)
        ),
    )(span_table, queries, flat)


def solution(mesh):
    in_specs = (P("ctx", "kvh", None), P(None, "ctx", "kvh", None), P())
    out_specs = P(("ctx", "kvh"), None)
    return jax.shard_map(body, mesh=mesh, in_specs=in_specs, out_specs=out_specs, check_vma=False)
```

```python
import functools
import math

import jax
import jax.numpy as jnp
from jax import lax
from jax.experimental import pallas as pl
from jax.experimental.pallas import tpu as pltpu
from jax.sharding import PartitionSpec as P

STEPS = 4
MESH = pl.DeviceIdType.MESH
LOW = -1e30
TILES = 4


def kernel(
    cycle,
    table_hbm,
    q_hbm,
    kv_hbm,
    out_ref,
    table_ref,
    q_in,
    kv_in,
    wide,
    qg,
    kvbuf,
    result,
    outbuf,
    load_sem,
    near_send,
    far_send,
    pass_send,
    kv_recv,
    out_send,
    out_recv,
    keep_sem,
    swap_sem,
):
    me = lax.axis_index("ctx")
    side = lax.axis_index("kvh")
    core = lax.rem(me, 2)
    rows, heads, hd = q_in.shape
    kvs = kvbuf.shape[0] - 1
    group = heads // kvs
    span = rows // 2
    tile_q = span // TILES
    tile_rows = tile_q * group
    width = group * hd
    factor = math.log2(math.e) / math.sqrt(hd)

    def ahead(n):
        return lax.rem(me + n + cycle, cycle)

    partner = me + 1 - 2 * core
    other = 1 - side

    load_kv = pltpu.make_async_copy(kv_hbm, kv_in, load_sem.at[0])
    load_kv.start()
    load_q = pltpu.make_async_copy(q_hbm, q_in, load_sem.at[1])
    load_q.start()
    load_table = pltpu.make_async_copy(table_hbm, table_ref, load_sem.at[2])
    load_table.start()

    barrier = pltpu.get_barrier_semaphore()
    pl.semaphore_signal(barrier, inc=1, device_id=(ahead(-2), side), device_id_type=MESH)
    pl.semaphore_signal(barrier, inc=1, device_id=(partner, side), device_id_type=MESH)
    pl.semaphore_signal(barrier, inc=1, device_id=(me, other), device_id_type=MESH)

    @pl.when(core == 0)
    def _():
        pl.semaphore_signal(barrier, inc=1, device_id=(ahead(-3), side), device_id_type=MESH)

    load_kv.wait()
    for part in range(2):
        wide[part] = kv_in[part].astype(jnp.float32)
    for g in range(kvs):
        for part in range(2):
            for s in range(2):
                kvbuf[g, part, s, 0] = wide[
                    part, pl.ds(s * span * kvs + g, span, stride=kvs), :
                ].astype(jnp.bfloat16)

    pl.semaphore_wait(barrier, 3 + core)

    far_slot = 1 + 2 * core
    pass_slot = 3 - 2 * core
    far_device = ahead(1 + 2 * core)

    def send_near(g):
        return pltpu.make_async_remote_copy(
            src_ref=kvbuf.at[g, :, :, 0],
            dst_ref=kvbuf.at[g, :, :, 2],
            send_sem=near_send.at[g],
            recv_sem=kv_recv.at[g, 2],
            device_id=(ahead(2), side),
            device_id_type=MESH,
        )

    def send_far(g):
        return pltpu.make_async_remote_copy(
            src_ref=kvbuf.at[g, :, :, 0],
            dst_ref=kvbuf.at[g, :, :, far_slot],
            send_sem=far_send.at[g],
            recv_sem=kv_recv.at[g, far_slot],
            device_id=(far_device, side),
            device_id_type=MESH,
        )

    def send_pass(g):
        return pltpu.make_async_remote_copy(
            src_ref=kvbuf.at[g, :, :, 2],
            dst_ref=kvbuf.at[g, :, :, pass_slot],
            send_sem=pass_send.at[g],
            recv_sem=kv_recv.at[g, pass_slot],
            device_id=(partner, side),
            device_id_type=MESH,
        )

    def arrival(g, slot):
        return pltpu.make_async_remote_copy(
            src_ref=kvbuf.at[g, :, :, 0],
            dst_ref=kvbuf.at[g, :, :, slot],
            send_sem=near_send.at[g],
            recv_sem=kv_recv.at[g, slot],
            device_id=(partner, side),
            device_id_type=MESH,
        )

    moved = kvs - 1
    moved_rows = pl.ds(pl.multiple_of(other * (span * group), span * group), span * group)
    swap_kv = pltpu.make_async_remote_copy(
        src_ref=kvbuf.at[moved, :, :, 0],
        dst_ref=kvbuf.at[kvs, :, :, 0],
        send_sem=swap_sem.at[0],
        recv_sem=swap_sem.at[1],
        device_id=(me, other),
        device_id_type=MESH,
    )
    swap_q = pltpu.make_async_remote_copy(
        src_ref=qg.at[moved, moved_rows],
        dst_ref=qg.at[kvs, moved_rows],
        send_sem=swap_sem.at[2],
        recv_sem=swap_sem.at[3],
        device_id=(me, other),
        device_id_type=MESH,
    )

    def columns(owner, g):
        return pl.ds(pl.multiple_of((owner * kvs + g) * width, width), width)

    def send_out(g):
        return pltpu.make_async_remote_copy(
            src_ref=outbuf.at[0, g],
            dst_ref=out_ref.at[:, columns(side, g)],
            send_sem=out_send.at[g],
            recv_sem=out_recv.at[g],
            device_id=(me, other),
            device_id_type=MESH,
        )

    def take_out(g):
        return pltpu.make_async_remote_copy(
            src_ref=outbuf.at[0, g],
            dst_ref=out_ref.at[:, columns(other, g)],
            send_sem=out_send.at[g],
            recv_sem=out_recv.at[g],
            device_id=(me, other),
            device_id_type=MESH,
        )

    def keep_out(g):
        return pltpu.make_async_copy(
            outbuf.at[1, g],
            out_ref.at[:, columns(jnp.where(g == kvs, other, side), jnp.minimum(g, moved))],
            keep_sem.at[g],
        )

    swap_kv.start()
    for g in range(kvs):
        send_near(g).start()
        send_far(g).start()

    load_q.wait()
    def regroup(g, s):
        for t in range(TILES):
            first = pl.multiple_of(s * span + t * tile_q, tile_q)
            block = q_in[pl.ds(first, tile_q)].astype(jnp.float32)
            qg[g, pl.ds(pl.multiple_of(first * group, tile_rows), tile_rows), :] = (
                block[:, g * group : (g + 1) * group, :]
                .reshape(tile_rows, hd)
                .astype(jnp.bfloat16)
            )

    regroup(moved, other)
    swap_q.start()
    regroup(moved, side)
    for g in range(kvs - 1):
        regroup(g, 0)
        regroup(g, 1)

    load_table.wait()
    biases = []
    for s in range(2):
        mine = table_ref[2 * me + s]
        biases.append(
            [None]
            + [
                jnp.where(table_ref[2 * ahead(-b) + s] < mine, 0.0, LOW).astype(jnp.float32)
                for b in range(1, STEPS)
            ]
        )

    def attend(g, late, slot):
        spans = 2 if late else 1
        keys = spans * STEPS * span

        def one(t, carry):
            start = pl.multiple_of(t * tile_rows, tile_rows)
            q = qg[g, pl.ds((span * group if late else 0) + start, tile_rows), :]
            k = kvbuf[g, 0, :spans].reshape(keys, hd)
            v = kvbuf[g, 1, :spans].reshape(keys, hd)
            scores = lax.dot_general(
                q, k, (((1,), (1,)), ((), ())), preferred_element_type=jnp.float32
            )
            parts = []
            for s in range(spans):
                for b in range(STEPS):
                    part = scores[:, (s * STEPS + b) * span : (s * STEPS + b + 1) * span]
                    if s == spans - 1:
                        if b == 0:
                            row = lax.broadcasted_iota(jnp.int32, part.shape, 0) // group
                            col = lax.broadcasted_iota(jnp.int32, part.shape, 1)
                            part = jnp.where(col <= row + t * tile_q, part, LOW)
                        else:
                            part = part + biases[s][b]
                    parts.append(part)
            top = functools.reduce(jnp.maximum, parts)
            top = jnp.max(top, axis=-1, keepdims=True)
            weights = jnp.concatenate(
                [jnp.exp2((part - top) * factor).astype(jnp.bfloat16) for part in parts], axis=1
            )
            both = jnp.dot(
                weights,
                jnp.concatenate([v, jnp.ones_like(v)], axis=1),
                preferred_element_type=jnp.float32,
            )
            result[pl.ds(start, tile_rows), :] = both[:, :hd] / both[:, hd:]
            first = pl.multiple_of(t * tile_q, tile_q)
            for h in range(group):
                outbuf[slot, g, pl.ds(first, tile_q), h * hd : (h + 1) * hd] = result[
                    pl.ds(start + h, tile_q, stride=group), :
                ].astype(jnp.bfloat16)
            return carry

        lax.fori_loop(0, TILES, one, 0, unroll=True)

    def compute(g, slot):
        late = jnp.where(slot == 0, other, side)

        @pl.when(late == 1)
        def _():
            attend(g, True, slot)

        @pl.when(late == 0)
        def _():
            attend(g, False, slot)

    swap_kv.wait_recv()
    send_near(kvs).start()
    send_far(kvs).start()
    arrival(0, 2).wait_recv()
    send_pass(0).start()
    pairs = 2 * (kvs - 1)

    def step(i, carry):
        g = jnp.where(i < pairs, i // 2, i - moved)
        slot = jnp.where(i < pairs, lax.rem(i, 2), 1)

        @pl.when(jnp.logical_or(slot == 0, i >= pairs))
        def _():
            arrival(g, 1).wait_recv()
            arrival(g, 3).wait_recv()

        @pl.when(jnp.logical_and(slot == 1, g < kvs))
        def _():
            arrival(g + 1, 2).wait_recv()
            send_pass(g + 1).start()

        @pl.when(g == kvs)
        def _():
            swap_q.wait_recv()

        compute(g, slot)

        @pl.when(slot == 0)
        def _():
            send_out(g).start()

        @pl.when(slot == 1)
        def _():
            keep_out(g).start()

        return carry

    lax.fori_loop(0, 2 * kvs, step, 0)

    swap_kv.wait_send()
    swap_q.wait_send()
    for g in range(kvs + 1):
        keep_out(g).wait()
        send_near(g).wait_send()
        send_far(g).wait_send()
        send_pass(g).wait_send()
    for g in range(moved):
        send_out(g).wait_send()
        take_out(g).wait_recv()


def body(queries, key_value, span_table):
    rows, heads, hd = queries.shape
    kvs = key_value.shape[2]
    group = heads // kvs
    span = rows // 2
    cycle = lax.axis_size("ctx")
    sides = lax.axis_size("kvh")
    flat = key_value.reshape(2, rows * kvs, hd)
    dma = pltpu.SemaphoreType.DMA
    flops = 3 * 2 * 2 * span * heads * STEPS * span * hd
    return pl.pallas_call(
        functools.partial(kernel, cycle),
        out_shape=jax.ShapeDtypeStruct((rows // sides, sides * heads * hd), jnp.bfloat16),
        in_specs=[
            pl.BlockSpec(memory_space=pl.ANY),
            pl.BlockSpec(memory_space=pl.ANY),
            pl.BlockSpec(memory_space=pl.ANY),
        ],
        out_specs=pl.BlockSpec(memory_space=pl.ANY),
        scratch_shapes=[
            pltpu.SMEM(span_table.shape, jnp.int32),
            pltpu.VMEM((rows, heads, hd), jnp.bfloat16),
            pltpu.VMEM((2, rows * kvs, hd), jnp.bfloat16),
            pltpu.VMEM((2, rows * kvs, hd), jnp.float32),
            pltpu.VMEM((kvs + 1, rows * group, hd), jnp.bfloat16),
            pltpu.VMEM((kvs + 1, 2, 2, STEPS, span, hd), jnp.bfloat16),
            pltpu.VMEM((span * group, hd), jnp.float32),
            pltpu.VMEM((2, kvs + 1, span, group * hd), jnp.bfloat16),
            dma((3,)),
            dma((kvs + 1,)),
            dma((kvs + 1,)),
            dma((kvs + 1,)),
            dma((kvs + 1, STEPS)),
            dma((kvs,)),
            dma((kvs,)),
            dma((kvs + 1,)),
            dma((4,)),
        ],
        compiler_params=pltpu.CompilerParams(
            collective_id=0, has_side_effects=True, vmem_limit_bytes=60 * 1024 * 1024
        ),
        cost_estimate=pl.CostEstimate(
            flops=flops, bytes_accessed=5 * 1024 * 1024, transcendentals=flops // (4 * hd)
        ),
    )(span_table, queries, flat)


def solution(mesh):
    in_specs = (P("ctx", "kvh", None), P(None, "ctx", "kvh", None), P())
    out_specs = P(("ctx", "kvh"), None)
    return jax.shard_map(body, mesh=mesh, in_specs=in_specs, out_specs=out_specs, check_vma=False)
```

```python
import functools
import math

import jax
import jax.numpy as jnp
from jax import lax
from jax.experimental import pallas as pl
from jax.experimental.pallas import tpu as pltpu
from jax.sharding import PartitionSpec as P

STEPS = 4
MESH = pl.DeviceIdType.MESH
LOW = -1e30
TILES = 4


def kernel(
    cycle,
    table_hbm,
    q_hbm,
    kv_hbm,
    out_ref,
    table_ref,
    q_in,
    kv_in,
    wide,
    qg,
    kvbuf,
    result,
    outbuf,
    load_sem,
    near_send,
    far_send,
    pass_send,
    kv_recv,
    out_send,
    out_recv,
    keep_sem,
    swap_sem,
):
    me = lax.axis_index("ctx")
    side = lax.axis_index("kvh")
    core = lax.rem(me, 2)
    rows, heads, hd = q_in.shape
    kvs = kvbuf.shape[0] - 1
    group = heads // kvs
    span = rows // 2
    tile_q = span // TILES
    tile_rows = tile_q * group
    width = group * hd
    factor = math.log2(math.e) / math.sqrt(hd)

    def ahead(n):
        return lax.rem(me + n + cycle, cycle)

    partner = me + 1 - 2 * core
    other = 1 - side

    load_kv = pltpu.make_async_copy(kv_hbm, kv_in, load_sem.at[0])
    load_kv.start()
    load_q = pltpu.make_async_copy(q_hbm, q_in, load_sem.at[1])
    load_q.start()
    load_table = pltpu.make_async_copy(table_hbm, table_ref, load_sem.at[2])
    load_table.start()

    barrier = pltpu.get_barrier_semaphore()
    pl.semaphore_signal(barrier, inc=1, device_id=(ahead(-2), side), device_id_type=MESH)
    pl.semaphore_signal(barrier, inc=1, device_id=(partner, side), device_id_type=MESH)
    pl.semaphore_signal(barrier, inc=1, device_id=(me, other), device_id_type=MESH)

    @pl.when(core == 0)
    def _():
        pl.semaphore_signal(barrier, inc=1, device_id=(ahead(-3), side), device_id_type=MESH)

    load_kv.wait()
    for part in range(2):
        wide[part] = kv_in[part].astype(jnp.float32)

    def split(g):
        for part in range(2):
            for s in range(2):
                kvbuf[g, part, s, 0] = wide[
                    part, pl.ds(s * span * kvs + g, span, stride=kvs), :
                ].astype(jnp.bfloat16)

    split(kvs - 1)
    split(0)
    pl.semaphore_wait(barrier, 3 + core)

    far_slot = 1 + 2 * core
    pass_slot = 3 - 2 * core
    far_device = ahead(1 + 2 * core)

    def send_near(g):
        return pltpu.make_async_remote_copy(
            src_ref=kvbuf.at[g, :, :, 0],
            dst_ref=kvbuf.at[g, :, :, 2],
            send_sem=near_send.at[g],
            recv_sem=kv_recv.at[g, 2],
            device_id=(ahead(2), side),
            device_id_type=MESH,
        )

    def send_far(g):
        return pltpu.make_async_remote_copy(
            src_ref=kvbuf.at[g, :, :, 0],
            dst_ref=kvbuf.at[g, :, :, far_slot],
            send_sem=far_send.at[g],
            recv_sem=kv_recv.at[g, far_slot],
            device_id=(far_device, side),
            device_id_type=MESH,
        )

    def send_pass(g):
        return pltpu.make_async_remote_copy(
            src_ref=kvbuf.at[g, :, :, 2],
            dst_ref=kvbuf.at[g, :, :, pass_slot],
            send_sem=pass_send.at[g],
            recv_sem=kv_recv.at[g, pass_slot],
            device_id=(partner, side),
            device_id_type=MESH,
        )

    def arrival(g, slot):
        return pltpu.make_async_remote_copy(
            src_ref=kvbuf.at[g, :, :, 0],
            dst_ref=kvbuf.at[g, :, :, slot],
            send_sem=near_send.at[g],
            recv_sem=kv_recv.at[g, slot],
            device_id=(partner, side),
            device_id_type=MESH,
        )

    moved = kvs - 1
    moved_rows = pl.ds(pl.multiple_of(other * (span * group), span * group), span * group)
    swap_kv = pltpu.make_async_remote_copy(
        src_ref=kvbuf.at[moved, :, :, 0],
        dst_ref=kvbuf.at[kvs, :, :, 0],
        send_sem=swap_sem.at[0],
        recv_sem=swap_sem.at[1],
        device_id=(me, other),
        device_id_type=MESH,
    )
    swap_q = pltpu.make_async_remote_copy(
        src_ref=qg.at[moved, moved_rows],
        dst_ref=qg.at[kvs, moved_rows],
        send_sem=swap_sem.at[2],
        recv_sem=swap_sem.at[3],
        device_id=(me, other),
        device_id_type=MESH,
    )

    def columns(owner, g):
        return pl.ds(pl.multiple_of((owner * kvs + g) * width, width), width)

    def send_out(g):
        return pltpu.make_async_remote_copy(
            src_ref=outbuf.at[0, g],
            dst_ref=out_ref.at[:, columns(side, g)],
            send_sem=out_send.at[g],
            recv_sem=out_recv.at[g],
            device_id=(me, other),
            device_id_type=MESH,
        )

    def take_out(g):
        return pltpu.make_async_remote_copy(
            src_ref=outbuf.at[0, g],
            dst_ref=out_ref.at[:, columns(other, g)],
            send_sem=out_send.at[g],
            recv_sem=out_recv.at[g],
            device_id=(me, other),
            device_id_type=MESH,
        )

    def keep_out(g):
        return pltpu.make_async_copy(
            outbuf.at[1, g],
            out_ref.at[:, columns(jnp.where(g == kvs, other, side), jnp.minimum(g, moved))],
            keep_sem.at[g],
        )

    swap_kv.start()
    send_near(0).start()
    send_far(0).start()
    load_q.wait()
    def regroup(g, s):
        for t in range(TILES):
            first = pl.multiple_of(s * span + t * tile_q, tile_q)
            block = q_in[pl.ds(first, tile_q)].astype(jnp.float32)
            qg[g, pl.ds(pl.multiple_of(first * group, tile_rows), tile_rows), :] = (
                block[:, g * group : (g + 1) * group, :]
                .reshape(tile_rows, hd)
                .astype(jnp.bfloat16)
            )

    regroup(moved, other)
    swap_q.start()
    for g in range(1, kvs):
        if g < moved:
            split(g)
        send_near(g).start()
        send_far(g).start()
    regroup(moved, side)
    for g in range(kvs - 1):
        regroup(g, 0)
        regroup(g, 1)

    load_table.wait()
    biases = []
    for s in range(2):
        mine = table_ref[2 * me + s]
        biases.append(
            [None]
            + [
                jnp.where(table_ref[2 * ahead(-b) + s] < mine, 0.0, LOW).astype(jnp.float32)
                for b in range(1, STEPS)
            ]
        )

    def attend(g, late, slot):
        spans = 2 if late else 1
        keys = spans * STEPS * span

        def one(t, carry):
            start = pl.multiple_of(t * tile_rows, tile_rows)
            q = qg[g, pl.ds((span * group if late else 0) + start, tile_rows), :]
            k = kvbuf[g, 0, :spans].reshape(keys, hd)
            v = kvbuf[g, 1, :spans].reshape(keys, hd)
            scores = lax.dot_general(
                q, k, (((1,), (1,)), ((), ())), preferred_element_type=jnp.float32
            )
            parts = []
            for s in range(spans):
                for b in range(STEPS):
                    part = scores[:, (s * STEPS + b) * span : (s * STEPS + b + 1) * span]
                    if s == spans - 1:
                        if b == 0:
                            row = lax.broadcasted_iota(jnp.int32, part.shape, 0) // group
                            col = lax.broadcasted_iota(jnp.int32, part.shape, 1)
                            part = jnp.where(col <= row + t * tile_q, part, LOW)
                        else:
                            part = part + biases[s][b]
                    parts.append(part)
            top = functools.reduce(jnp.maximum, parts)
            top = jnp.max(top, axis=-1, keepdims=True)
            weights = jnp.concatenate(
                [jnp.exp2((part - top) * factor).astype(jnp.bfloat16) for part in parts], axis=1
            )
            both = jnp.dot(
                weights,
                jnp.concatenate([v, jnp.ones_like(v)], axis=1),
                preferred_element_type=jnp.float32,
            )
            result[pl.ds(start, tile_rows), :] = both[:, :hd] / both[:, hd:]
            first = pl.multiple_of(t * tile_q, tile_q)
            for h in range(group):
                outbuf[slot, g, pl.ds(first, tile_q), h * hd : (h + 1) * hd] = result[
                    pl.ds(start + h, tile_q, stride=group), :
                ].astype(jnp.bfloat16)
            return carry

        lax.fori_loop(0, TILES, one, 0, unroll=True)

    def compute(g, slot):
        late = jnp.where(slot == 0, other, side)

        @pl.when(late == 1)
        def _():
            attend(g, True, slot)

        @pl.when(late == 0)
        def _():
            attend(g, False, slot)

    swap_kv.wait_recv()
    send_near(kvs).start()
    send_far(kvs).start()
    arrival(0, 2).wait_recv()
    send_pass(0).start()
    pairs = 2 * (kvs - 1)

    def step(i, carry):
        g = jnp.where(i < pairs, i // 2, i - moved)
        slot = jnp.where(i < pairs, lax.rem(i, 2), 1)

        @pl.when(jnp.logical_or(slot == 0, i >= pairs))
        def _():
            arrival(g, 1).wait_recv()
            arrival(g, 3).wait_recv()

        @pl.when(jnp.logical_and(slot == 1, g < kvs))
        def _():
            arrival(g + 1, 2).wait_recv()
            send_pass(g + 1).start()

        @pl.when(g == kvs)
        def _():
            swap_q.wait_recv()

        compute(g, slot)

        @pl.when(slot == 0)
        def _():
            send_out(g).start()

        @pl.when(slot == 1)
        def _():
            keep_out(g).start()

        return carry

    lax.fori_loop(0, 2 * kvs, step, 0)

    swap_kv.wait_send()
    swap_q.wait_send()
    for g in range(kvs + 1):
        keep_out(g).wait()
        send_near(g).wait_send()
        send_far(g).wait_send()
        send_pass(g).wait_send()
    for g in range(moved):
        send_out(g).wait_send()
        take_out(g).wait_recv()


def body(queries, key_value, span_table):
    rows, heads, hd = queries.shape
    kvs = key_value.shape[2]
    group = heads // kvs
    span = rows // 2
    cycle = lax.axis_size("ctx")
    sides = lax.axis_size("kvh")
    flat = key_value.reshape(2, rows * kvs, hd)
    dma = pltpu.SemaphoreType.DMA
    flops = 3 * 2 * 2 * span * heads * STEPS * span * hd
    return pl.pallas_call(
        functools.partial(kernel, cycle),
        out_shape=jax.ShapeDtypeStruct((rows // sides, sides * heads * hd), jnp.bfloat16),
        in_specs=[
            pl.BlockSpec(memory_space=pl.ANY),
            pl.BlockSpec(memory_space=pl.ANY),
            pl.BlockSpec(memory_space=pl.ANY),
        ],
        out_specs=pl.BlockSpec(memory_space=pl.ANY),
        scratch_shapes=[
            pltpu.SMEM(span_table.shape, jnp.int32),
            pltpu.VMEM((rows, heads, hd), jnp.bfloat16),
            pltpu.VMEM((2, rows * kvs, hd), jnp.bfloat16),
            pltpu.VMEM((2, rows * kvs, hd), jnp.float32),
            pltpu.VMEM((kvs + 1, rows * group, hd), jnp.bfloat16),
            pltpu.VMEM((kvs + 1, 2, 2, STEPS, span, hd), jnp.bfloat16),
            pltpu.VMEM((span * group, hd), jnp.float32),
            pltpu.VMEM((2, kvs + 1, span, group * hd), jnp.bfloat16),
            dma((3,)),
            dma((kvs + 1,)),
            dma((kvs + 1,)),
            dma((kvs + 1,)),
            dma((kvs + 1, STEPS)),
            dma((kvs,)),
            dma((kvs,)),
            dma((kvs + 1,)),
            dma((4,)),
        ],
        compiler_params=pltpu.CompilerParams(
            collective_id=0, has_side_effects=True, vmem_limit_bytes=int(51 * 1024 * 1024)
        ),
        cost_estimate=pl.CostEstimate(
            flops=flops, bytes_accessed=5 * 1024 * 1024, transcendentals=flops // (4 * hd)
        ),
    )(span_table, queries, flat)


def solution(mesh):
    in_specs = (P("ctx", "kvh", None), P(None, "ctx", "kvh", None), P())
    out_specs = P(("ctx", "kvh"), None)
    return jax.shard_map(body, mesh=mesh, in_specs=in_specs, out_specs=out_specs, check_vma=False)
```
